32 devices in a mesh: groups: 2 (over y), pool: 4 (over z), tensor: 4 (over x, core).
Axes of the slice: x: 2, y: 2, z: 4, core: 2. Of those that a mesh axis runs over, the one named last changes fastest.
Arguments:
- prompt_query: bfloat16 [2048, 8192], P(('groups', 'pool'), 'tensor'), parts along dimension 0, may hold values from -20 to 20
- prompt_key_value: bfloat16 [2048, 8, 256], P(('groups', 'pool'), 'tensor'), parts along dimension 0, may hold values from -20 to 20
- segment_ids: int32 [2048], P('groups'), parts along dimension 0, may hold values from 0 to 2, never falling along the last dimension, each value on 1 to 512 neighbouring positions
- block_dest: int32 [128, 1], P('groups'), parts along dimension 0, may hold values from 0 to 3; in each aligned block of 16 rows (0 to 15, 16 to 31, ...) at most 8 rows name the same one
- decode_query: bfloat16 [2, 192, 8192], P(None, ('groups', 'pool'), 'tensor'), parts along dimension 1, may hold values from -20 to 20
- dec_kv: bfloat16 [2, 192, 8, 256], P(None, ('groups', 'pool'), 'tensor'), parts along dimension 1, may hold values from -20 to 20
- dec_cache: bfloat16 [192, 512, 8, 256], P(('groups', 'pool'), None, 'tensor'), parts along dimension 0, may hold values from -20 to 20
- ctx_len: int32 [192], P(('groups', 'pool')), parts along dimension 0, may hold values from 1 to 512, 24576 in all
- out_weight: bfloat16 [8192, 8192], P('tensor', 'pool'), may hold values from -0.0625 to 0.0625
Outputs:
- prefill_out: bfloat16 [2048, 8192], P(('groups', 'tensor'), 'pool'), parts along dimension 0
- decode_out: bfloat16 [2, 192, 8192], P(None, ('groups', 'tensor'), 'pool'), parts along dimension 1
- arrived: bfloat16 [8, 4, 8, 16, 8, 256], P(('groups', 'pool'), None, None, None, 'tensor'), parts along dimension 0
The draws below stay inside these ranges and needn't reach their ends.
There are 2 independent parts, one for each index of `groups`. The reference program is written for one: setup_inputs(seed, part) draws one part's arguments, and reference() takes and returns one part's arrays. A program takes and returns all parts, laid end to end along the dimension named above; an argument that names none is the same for every part. Nothing has to cross between parts.
Inputs may be any that keep to these rules, and one draw needn't show every extreme that they name: `segment_ids`: prompts never fall back to an earlier id; a prompt has at most 512 tokens and one has exactly 512. `block_dest`: among the 16 blocks of one member, at most 8 go to one receiver. `ctx_len`: one request has exactly 512 cached tokens.
All inputs are finite; a program needn't handle non-finite values. No bound on the sum of `ctx_len` on one device may be relied on, other than what follows from the above.
Results may differ from the reference program's by a relative error of at most 0.012.
Values may be sent and summed in bfloat16 or wider, within the bound.
A program may use at most 128 MiB of HBM per device.

```python
import math
import jax
import jax.numpy as jnp
import numpy as np
from jax import lax

D = 8192
QUERY_HEAD_COUNT = 64
KEY_HEADS = 8
HEAD_WIDTH = 128
BLOCK_TOKENS = 16
PRE_DEV = 256
DECODE_SLOTS = 512
MEMBER_BLOCKS = 16
RECEIVER_SLOTS = 8
PROMPT_TOKENS = 1024
MOST = 512
DECODE_REQUESTS = 96
BLOCKS = 64
N_POOL = 4


def draw_prompt_query(key, part):
    key = jax.random.fold_in(key, 1)
    key_values = jax.random.fold_in(key, 0)
    tensor_shape = (PROMPT_TOKENS, KEY_HEADS, QUERY_HEAD_COUNT // KEY_HEADS, HEAD_WIDTH)
    values = jnp.clip(jax.random.normal(key_values, tensor_shape, jnp.float32), -6.0, 6.0)
    return values.reshape(PROMPT_TOKENS, QUERY_HEAD_COUNT * HEAD_WIDTH).astype(jnp.bfloat16)


def draw_prompt_key_value(key, part):
    key = jax.random.fold_in(key, 2)
    key_values = jax.random.fold_in(key, 0)
    tensor_shape = (PROMPT_TOKENS, KEY_HEADS, 2 * HEAD_WIDTH)
    values = jnp.clip(jax.random.normal(key_values, tensor_shape, jnp.float32), -6.0, 6.0)
    return values.astype(jnp.bfloat16)


def draw_decode_query(key, part):
    key = jax.random.fold_in(key, 3)
    key_values = jax.random.fold_in(key, 0)
    tensor_shape = (2, DECODE_REQUESTS, KEY_HEADS, QUERY_HEAD_COUNT // KEY_HEADS, HEAD_WIDTH)
    values = jnp.clip(jax.random.normal(key_values, tensor_shape, jnp.float32), -6.0, 6.0)
    return values.reshape(2, DECODE_REQUESTS, QUERY_HEAD_COUNT * HEAD_WIDTH).astype(jnp.bfloat16)


def draw_dec_kv(key, part):
    key = jax.random.fold_in(key, 4)
    key_values = jax.random.fold_in(key, 0)
    tensor_shape = (2, DECODE_REQUESTS, KEY_HEADS, 2 * HEAD_WIDTH)
    values = jnp.clip(jax.random.normal(key_values, tensor_shape, jnp.float32), -6.0, 6.0)
    return values.astype(jnp.bfloat16)


def draw_dec_cache(key, part):
    key = jax.random.fold_in(key, 5)
    key_values = jax.random.fold_in(key, 0)
    tensor_shape = (DECODE_REQUESTS, DECODE_SLOTS, KEY_HEADS, 2 * HEAD_WIDTH)
    values = jnp.clip(jax.random.normal(key_values, tensor_shape, jnp.float32), -6.0, 6.0)
    return values.astype(jnp.bfloat16)


def shard_levels(stream_key, dims, cuts, least, high):
    gain = 1.0
    for axis_at, parts in cuts:
        draws = jax.random.uniform(jax.random.fold_in(jax.random.fold_in(stream_key, 6), axis_at), (parts,), jnp.float32, least / len(cuts), high / len(cuts))
        gain = gain * jnp.repeat(jnp.exp(draws), dims[axis_at] // parts).reshape((-1,) + (1,) * (len(dims) - 1 - axis_at))
    return gain


def length_profile(amount, total, limit, lean):
    portions = [(1 << 20) // math.isqrt(grade ** lean) + 1 for grade in range(2, amount + 1)]
    surplus, counts = total - limit - (amount - 1), [1] * (amount - 1)
    while surplus > 0:
        free = [i for i in range(amount - 1) if counts[i] < limit]
        whole, remaining = sum([portions[i] for i in free]), surplus
        for i in free:
            extra = min(limit - counts[i], max(1, remaining * portions[i] // whole), surplus)
            counts[i] = counts[i] + extra
            surplus = surplus - extra
    return np.array([limit] + counts)


def uneven_parts(stream_key, count, total, most, slope):
    if count == 2:
        one = jax.random.randint(stream_key, (), max(1, total - most), min(most, total - 1) + 1)
        return jnp.stack([one, total - one])
    sizes = jnp.asarray(length_profile(count, total, most, slope), jnp.int32)
    twos = (count - 1) // 2
    source_of, taker = sizes[1:1 + 2 * twos:2], sizes[2:2 + 2 * twos:2]
    room = jnp.minimum(source_of - 1, most - taker)
    shifted = jax.random.randint(jax.random.fold_in(stream_key, 1), (twos,), 0, 1 << 20) % (room + 1)
    sizes = sizes.at[1:1 + 2 * twos:2].set(source_of - shifted).at[2:2 + 2 * twos:2].set(taker + shifted)
    return sizes[jax.random.permutation(jax.random.fold_in(stream_key, 2), count)]


def routed_block(stream_key, own, number, rows, amount, top, bound, slope):
    ranking = jax.random.permutation(stream_key, amount)
    packed, ordinary = shares(amount, rows * top, bound, slope, True), shares(amount, rows * top, bound, slope, False)
    places = jnp.arange(amount)

    def named(tallies, turn):
        used = int((tallies > 0).sum())
        fixed = max(1, used // 4)
        passed = fixed + (places - fixed + turn * (used - fixed)) % max(1, amount - fixed)
        return jnp.zeros((amount,), jnp.int32).at[ranking[jnp.where(places < fixed, places, passed)]].set(jnp.asarray(tallies, jnp.int32))

    tallies = jnp.where(number % 4 == 0, named(packed, number // 4), named(ordinary, number - number // 4 - 1))
    mixed = jax.random.permutation(jax.random.fold_in(own, 3), amount)
    source_of, sink = mixed[0:amount // 2 * 2:2], mixed[1:amount // 2 * 2:2]
    room = jnp.minimum(tallies[source_of] - 1, bound - tallies[sink]) // 2
    room = jnp.where((source_of == ranking[0]) | (sink == ranking[0]) | (tallies[sink] == 0), 0, jnp.maximum(room, 0))
    passed = jax.random.randint(jax.random.fold_in(own, 4), (amount // 2,), 0, 1 << 20) % (room + 1)
    tallies = tallies.at[source_of].add(-passed).at[sink].add(passed)
    items = jnp.searchsorted(jnp.cumsum(tallies), jnp.arange(rows * top), side="right").astype(jnp.int32)
    listing = items.reshape(top, rows).T
    listing = listing[jax.random.permutation(jax.random.fold_in(own, 1), rows)]
    turn = jax.random.randint(jax.random.fold_in(own, 2), (rows, 1), 0, top)
    return jnp.take_along_axis(listing, (jnp.arange(top)[None, :] + turn) % top, axis=1)


def shares(count, total, limit, slope, full):
    weights = [(1 << 20) // math.isqrt(grade ** slope) + 1 for grade in range(1, count + 1)]
    largest = limit if full else min(limit, max(-(-total // count), total * weights[0] // sum(weights)))
    least = 1 if total - largest >= count - 1 else 0
    given, spare = [largest] + [least] * (count - 1), total - largest - least * (count - 1)
    while spare > 0:
        movable = [i for i in range(1, count) if given[i] < largest] or [i for i in range(1, count) if given[i] < limit]
        whole, remaining = sum([weights[i] for i in movable]), spare
        for i in movable:
            extra = min(limit - given[i], max(1, remaining * weights[i] // whole), spare)
            given[i] = given[i] + extra
            spare = spare - extra
    return np.array(given)


def gaussian(rng, dims, scale, reach, pieces=(), kind=jnp.bfloat16):
    values = jax.random.normal(rng, dims, jnp.float32) * scale
    if len(pieces) > 0:
        values = shard_levels(rng, dims, pieces, -0.22, 0.18) * values
    return jnp.clip(values, min=-reach, max=reach).astype(kind)


def setup_inputs(seed: int = 0, part: int = 0) -> dict:
    key_list = jax.random.split(jax.random.key(seed), 10)
    part_keys = jax.random.split(jax.random.fold_in(key_list[9], part), 10)
    prompt_query = draw_prompt_query(jax.random.fold_in(jax.random.fold_in(key_list[9], part), 71), part)
    prompt_key_value = draw_prompt_key_value(jax.random.fold_in(jax.random.fold_in(key_list[9], part), 71), part)
    segment_ids = jnp.searchsorted(jnp.cumsum(uneven_parts(part_keys[2], 3, PROMPT_TOKENS, MOST, 2)), jnp.arange(PROMPT_TOKENS), side="right").astype(jnp.int32)
    block_dest_keys = jax.random.split(jax.random.fold_in(part_keys[3], 1), BLOCKS // MEMBER_BLOCKS)
    block_dest_turns = jax.random.permutation(jax.random.fold_in(part_keys[3], 3), BLOCKS // MEMBER_BLOCKS)
    block_dest = jax.vmap(lambda own, number: routed_block(jax.random.fold_in(part_keys[3], 2), own, number, MEMBER_BLOCKS, N_POOL, 1, RECEIVER_SLOTS, 2))(block_dest_keys, block_dest_turns).reshape((BLOCKS, 1))
    decode_query = draw_decode_query(jax.random.fold_in(jax.random.fold_in(key_list[9], part), 71), part)
    dec_kv = draw_dec_kv(jax.random.fold_in(jax.random.fold_in(key_list[9], part), 71), part)
    dec_cache = draw_dec_cache(jax.random.fold_in(jax.random.fold_in(key_list[9], part), 71), part)
    ctx_len = uneven_parts(part_keys[7], DECODE_REQUESTS, DECODE_REQUESTS * DECODE_SLOTS // 2, DECODE_SLOTS, 2).astype(jnp.int32)
    out_weight = gaussian(key_list[8], (QUERY_HEAD_COUNT * HEAD_WIDTH, D), (QUERY_HEAD_COUNT * HEAD_WIDTH) ** -0.5, 0.0625, ((0, 4), (1, 4)))
    return {"prompt_query": prompt_query, "prompt_key_value": prompt_key_value, "segment_ids": segment_ids, "block_dest": block_dest, "decode_query": decode_query, "dec_kv": dec_kv, "dec_cache": dec_cache, "ctx_len": ctx_len, "out_weight": out_weight}


def block_ranks(destinations):
    item_count = destinations.shape[-1]
    same_dest = destinations[..., :, None] == destinations[..., None, :]
    earlier = jnp.arange(item_count, dtype=jnp.int32)[None, :] < jnp.arange(item_count, dtype=jnp.int32)[:, None]
    return lax.optimization_barrier(jnp.sum(jnp.where(same_dest & earlier, 1, 0), axis=-1)).astype(jnp.int32)

def reference(prompt_query, prompt_key_value, segment_ids, block_dest, decode_query, dec_kv, dec_cache, ctx_len, out_weight):
    query_group_width = QUERY_HEAD_COUNT // KEY_HEADS
    score_scale = 1.0 / math.sqrt(HEAD_WIDTH)
    positions = jnp.arange(PROMPT_TOKENS, dtype=jnp.int32)
    query_matrix = prompt_query.reshape(PROMPT_TOKENS, KEY_HEADS, query_group_width, HEAD_WIDTH).transpose(1, 0, 2, 3)
    stacked = prompt_key_value.transpose(1, 0, 2)
    block_count = PROMPT_TOKENS // PRE_DEV

    def prompt_head(operands):
        head_q, head_kv = operands
        head_keys = head_kv[:, :HEAD_WIDTH].astype(jnp.float32)
        head_values = head_kv[:, HEAD_WIDTH:].astype(jnp.float32)

        def query_block(block_index):
            first_row = (block_index * PRE_DEV).astype(jnp.int32)
            block_q = lax.dynamic_slice_in_dim(head_q, first_row, PRE_DEV, 0).astype(jnp.float32)
            block_pos = first_row + jnp.arange(PRE_DEV, dtype=jnp.int32)
            block_seg = lax.dynamic_slice_in_dim(segment_ids, first_row, PRE_DEV, 0)
            scores = jnp.einsum('tgd,sd->tgs', block_q, head_keys) * score_scale
            allowed = (block_seg[:, None] == segment_ids[None, :]) & (positions[None, :] <= block_pos[:, None])
            allowed = allowed[:, None, :]
            row_max = lax.optimization_barrier(jnp.max(jnp.where(allowed, scores, -1e+30), axis=-1, keepdims=True))
            weights = jnp.where(allowed, jnp.exp(scores - row_max), 0.0)
            weight_total = lax.optimization_barrier(jnp.sum(weights, axis=-1, keepdims=True))
            rounded = lax.optimization_barrier(weights.astype(jnp.bfloat16)).astype(jnp.float32)
            return jnp.einsum('tgs,sd->tgd', rounded, head_values) / weight_total
        return lax.map(query_block, jnp.arange(block_count, dtype=jnp.int32)).reshape(PROMPT_TOKENS, query_group_width, HEAD_WIDTH)
    prompt = lax.map(prompt_head, (query_matrix, stacked))
    pre_att = prompt.transpose(1, 0, 2, 3).reshape(PROMPT_TOKENS, QUERY_HEAD_COUNT * HEAD_WIDTH).astype(jnp.bfloat16)
    decode_query_rows = decode_query.reshape(2, DECODE_REQUESTS, KEY_HEADS, query_group_width, HEAD_WIDTH).transpose(2, 0, 1, 3, 4)
    dec_new = dec_kv.transpose(2, 0, 1, 3)
    dec_old = dec_cache.transpose(2, 0, 1, 3)
    live_mask = (jnp.arange(DECODE_SLOTS, dtype=jnp.int32)[None, :] < ctx_len[:, None])[:, None, :]

    def decode_head(operands):
        head_q, head_new, head_old = operands
        old_keys = head_old[..., :HEAD_WIDTH].astype(jnp.float32)
        old_values = head_old[..., HEAD_WIDTH:].astype(jnp.float32)
        new_keys = head_new[..., :HEAD_WIDTH].astype(jnp.float32)
        new_values = head_new[..., HEAD_WIDTH:].astype(jnp.float32)
        outputs = []
        for step_index in range(2):
            query_rows = head_q[step_index].astype(jnp.float32)
            old_scores = jnp.einsum('rgd,rcd->rgc', query_rows, old_keys) * score_scale
            new_scores = jnp.einsum('rgd,nrd->rgn', query_rows, new_keys[:step_index + 1]) * score_scale
            row_max = jnp.maximum(lax.optimization_barrier(jnp.max(jnp.where(live_mask, old_scores, -1e+30), axis=-1, keepdims=True)), lax.optimization_barrier(jnp.max(new_scores, axis=-1, keepdims=True)))
            old_weights = jnp.where(live_mask, jnp.exp(old_scores - row_max), 0.0)
            new_weights = jnp.exp(new_scores - row_max)
            weight_total = lax.optimization_barrier(jnp.sum(old_weights, axis=-1, keepdims=True)) + lax.optimization_barrier(jnp.sum(new_weights, axis=-1, keepdims=True))
            old_round = lax.optimization_barrier(old_weights.astype(jnp.bfloat16)).astype(jnp.float32)
            new_round = lax.optimization_barrier(new_weights.astype(jnp.bfloat16)).astype(jnp.float32)
            combined = jnp.einsum('rgc,rcd->rgd', old_round, old_values) + jnp.einsum('rgn,nrd->rgd', new_round, new_values[:step_index + 1])
            outputs.append(combined / weight_total)
        return jnp.stack(outputs)
    decoded = lax.map(decode_head, (decode_query_rows, dec_new, dec_old))
    dec_att = decoded.transpose(1, 2, 0, 3, 4).reshape(2, DECODE_REQUESTS, QUERY_HEAD_COUNT * HEAD_WIDTH).astype(jnp.bfloat16)
    prefill_out = jnp.dot(pre_att, out_weight, preferred_element_type=jnp.float32).astype(jnp.bfloat16)
    decode_out = jnp.dot(dec_att.reshape(2 * DECODE_REQUESTS, QUERY_HEAD_COUNT * HEAD_WIDTH), out_weight, preferred_element_type=jnp.float32)
    decode_out = decode_out.reshape(2, DECODE_REQUESTS, D).astype(jnp.bfloat16)
    destinations = block_dest[:, 0].reshape(N_POOL, MEMBER_BLOCKS)
    slot_ranks = block_ranks(destinations)
    cache_blocks = prompt_key_value.reshape(N_POOL, MEMBER_BLOCKS, BLOCK_TOKENS * KEY_HEADS * 2 * HEAD_WIDTH).astype(jnp.float32)
    receivers = jnp.arange(N_POOL, dtype=jnp.int32)
    slot_ids = jnp.arange(RECEIVER_SLOTS, dtype=jnp.int32)
    select_entries = ((destinations[None, :, None, :] == receivers[:, None, None, None]) & (slot_ranks[None, :, None, :] == slot_ids[None, None, :, None])).astype(jnp.float32)
    arrived = jnp.einsum('towg,oge->towe', select_entries, cache_blocks).reshape(N_POOL, N_POOL, RECEIVER_SLOTS, BLOCK_TOKENS, KEY_HEADS, 2 * HEAD_WIDTH).astype(jnp.bfloat16)
    return (prefill_out, decode_out, arrived)
```

```python
import functools
import math

import jax
import jax.numpy as jnp
from jax import lax
from jax.experimental import pallas as pl
from jax.experimental.pallas import tpu as pltpu
from jax.sharding import PartitionSpec as P

BLOCK_TOKENS = 16
MESH = pl.DeviceIdType.MESH
COLUMN_TILE = 512


def project_kernel(
    chunks,
    slot_members,
    att_ref,
    weight_ref,
    out_ref,
    gathered,
    weight,
    outgoing,
    landed,
    total,
    own_sem,
    weight_sem,
    ring_send,
    ring_recv,
    part_send,
    part_recv,
):
    pool = lax.axis_size("pool")
    tensor = lax.axis_size("tensor")
    group = lax.axis_index("groups")
    me = lax.axis_index("pool")
    lane = lax.axis_index("tensor")
    columns = weight_ref.shape[1]
    tile = min(COLUMN_TILE, columns)
    has_left = me > 0
    has_right = me < pool - 1

    load_weight = pltpu.make_async_copy(weight_ref, weight, weight_sem)
    load_weight.start()
    load_own = pltpu.make_async_copy(att_ref, gathered.at[me], own_sem)
    load_own.start()

    barrier = pltpu.get_barrier_semaphore()

    @pl.when(has_left)
    def _():
        pl.semaphore_signal(barrier, inc=1, device_id=(group, me - 1, lane), device_id_type=MESH)

    @pl.when(has_right)
    def _():
        pl.semaphore_signal(barrier, inc=1, device_id=(group, me + 1, lane), device_id_type=MESH)

    for step in range(1, tensor):
        peer = lax.rem(lane + step, tensor)
        pl.semaphore_signal(barrier, inc=1, device_id=(group, me, peer), device_id_type=MESH)

    pl.semaphore_wait(
        barrier, has_left.astype(jnp.int32) + has_right.astype(jnp.int32) + tensor - 1
    )

    def ring_copy(member, chunk, way):
        start, size = chunks[chunk]
        block = gathered.at[member, pl.ds(start, size)]
        return pltpu.make_async_remote_copy(
            src_ref=block,
            dst_ref=block,
            send_sem=ring_send.at[way, member, chunk],
            recv_sem=ring_recv.at[member, chunk],
            device_id=(group, me - 1 if way == 0 else me + 1, lane),
            device_id_type=MESH,
        )

    def part_copy(member, chunk):
        start, size = chunks[chunk]
        target = member // slot_members
        return pltpu.make_async_remote_copy(
            src_ref=outgoing.at[member, pl.ds(start, size)],
            dst_ref=landed.at[lane, member % slot_members, pl.ds(start, size)],
            send_sem=part_send.at[member, chunk],
            recv_sem=part_recv.at[lane, member % slot_members, chunk],
            device_id=(group, me, target),
            device_id_type=MESH,
        )

    def arrived_copy(source, place, chunk):
        start, size = chunks[chunk]
        return pltpu.make_async_remote_copy(
            src_ref=outgoing.at[0, pl.ds(start, size)],
            dst_ref=landed.at[source, place, pl.ds(start, size)],
            send_sem=part_send.at[0, chunk],
            recv_sem=part_recv.at[source, place, chunk],
            device_id=(group, me, source),
            device_id_type=MESH,
        )

    def project(member, chunk):
        start, size = chunks[chunk]
        mine = member // slot_members == lane

        @pl.loop(0, columns // tile)
        def _(index):
            place = pl.ds(pl.multiple_of(index * tile, tile), tile)
            part = jnp.dot(
                gathered[member, pl.ds(start, size), :],
                weight[:, place],
                preferred_element_type=jnp.float32,
            )

            @pl.when(mine)
            def _():
                total[member % slot_members, pl.ds(start, size), place] = part

            @pl.when(jnp.logical_not(mine))
            def _():
                outgoing[member, pl.ds(start, size), place] = part.astype(jnp.bfloat16)

        @pl.when(jnp.logical_not(mine))
        def _():
            part_copy(member, chunk).start()

    load_own.wait()
    for chunk in range(len(chunks)):
        @pl.when(has_left)
        def _():
            ring_copy(me, chunk, 0).start()

        @pl.when(has_right)
        def _():
            ring_copy(me, chunk, 1).start()

    load_weight.wait()

    @pl.loop(0, pool)
    def _(distance):
        left = me - distance
        right = me + distance
        use_left = left >= 0
        use_right = jnp.logical_and(right < pool, distance > 0)
        for chunk in range(len(chunks)):
            @pl.when(jnp.logical_and(use_left, distance > 0))
            def _():
                ring_copy(left, chunk, 1).wait_recv()

                @pl.when(has_right)
                def _():
                    ring_copy(left, chunk, 1).start()

            @pl.when(use_right)
            def _():
                ring_copy(right, chunk, 0).wait_recv()

                @pl.when(has_left)
                def _():
                    ring_copy(right, chunk, 0).start()

            @pl.when(use_left)
            def _():
                project(left, chunk)

            @pl.when(use_right)
            def _():
                project(right, chunk)

    for place in range(slot_members):
        for chunk in range(len(chunks)):
            start, size = chunks[chunk]
            for step in range(1, tensor):
                arrived_copy(lax.rem(lane + step, tensor), place, chunk).wait_recv()

            @pl.loop(0, columns // tile)
            def _(index):
                span = pl.ds(pl.multiple_of(index * tile, tile), tile)
                value = total[place, pl.ds(start, size), span]
                for step in range(1, tensor):
                    source = lax.rem(lane + step, tensor)
                    value = value + landed[source, place, pl.ds(start, size), span].astype(
                        jnp.float32
                    )
                out_ref[place, pl.ds(start, size), span] = value.astype(jnp.bfloat16)

    @pl.loop(0, pool)
    def _(member):
        for chunk in range(len(chunks)):
            @pl.when(jnp.logical_and(has_left, member >= me))
            def _():
                ring_copy(member, chunk, 0).wait_send()

            @pl.when(jnp.logical_and(has_right, member <= me))
            def _():
                ring_copy(member, chunk, 1).wait_send()

            @pl.when(member // slot_members != lane)
            def _():
                part_copy(member, chunk).wait_send()


def project_all(att, out_weight, chunks):
    pool = lax.axis_size("pool")
    tensor = lax.axis_size("tensor")
    rows, depth = att.shape
    columns = out_weight.shape[1]
    slot_members = pool // tensor
    count = len(chunks)
    return pl.pallas_call(
        functools.partial(project_kernel, chunks, slot_members),
        out_shape=jax.ShapeDtypeStruct((slot_members, rows, columns), jnp.bfloat16),
        in_specs=[pl.BlockSpec(memory_space=pl.ANY)] * 2,
        out_specs=pl.BlockSpec(memory_space=pltpu.VMEM),
        scratch_shapes=[
            pltpu.VMEM((pool, rows, depth), jnp.bfloat16),
            pltpu.VMEM((depth, columns), jnp.bfloat16),
            pltpu.VMEM((pool, rows, columns), jnp.bfloat16),
            pltpu.VMEM((tensor, slot_members, rows, columns), jnp.bfloat16),
            pltpu.VMEM((slot_members, rows, columns), jnp.float32),
            pltpu.SemaphoreType.DMA,
            pltpu.SemaphoreType.DMA,
            pltpu.SemaphoreType.DMA((2, pool, count)),
            pltpu.SemaphoreType.DMA((pool, count)),
            pltpu.SemaphoreType.DMA((pool, count)),
            pltpu.SemaphoreType.DMA((tensor, slot_members, count)),
        ],
        compiler_params=pltpu.CompilerParams(
            collective_id=0, has_side_effects=True, vmem_limit_bytes=50 * 1024 * 1024
        ),
        cost_estimate=pl.CostEstimate(
            flops=2 * pool * rows * depth * columns,
            bytes_accessed=2 * (depth * columns + 2 * rows * depth),
            transcendentals=0,
        ),
    )(att, out_weight)


def block_ranks(destinations):
    item_count = destinations.shape[-1]
    same_dest = destinations[..., :, None] == destinations[..., None, :]
    earlier = (
        jnp.arange(item_count, dtype=jnp.int32)[None, :]
        < jnp.arange(item_count, dtype=jnp.int32)[:, None]
    )
    return jnp.sum(jnp.where(same_dest & earlier, 1, 0), axis=-1).astype(jnp.int32)


def body(
    prompt_query,
    prompt_key_value,
    segment_ids,
    block_dest,
    decode_query,
    dec_kv,
    dec_cache,
    ctx_len,
    out_weight,
):
    row_count = prompt_query.shape[0]
    kv_heads = prompt_key_value.shape[1]
    head_size = prompt_key_value.shape[2] // 2
    query_heads = prompt_query.shape[1] // head_size
    query_group_width = query_heads // kv_heads
    score_scale = 1.0 / math.sqrt(head_size)
    pool_size = lax.axis_size("pool")
    my_index = lax.axis_index("pool")
    own_start = my_index * row_count
    own_positions = own_start + jnp.arange(row_count, dtype=jnp.int32)
    own_segments = lax.dynamic_slice_in_dim(segment_ids, own_start, row_count, 0)
    query_matrix = prompt_query.reshape(row_count, kv_heads, query_group_width, head_size)
    block_size = BLOCK_TOKENS
    block_count = row_count // block_size
    capacity = max(2, 2 * block_count // pool_size)
    destinations = block_dest[:, 0].reshape(pool_size, block_count)
    slot_ranks = block_ranks(destinations)
    flat_size = block_size * kv_heads * 2 * head_size
    slot_ids = jnp.arange(capacity, dtype=jnp.int32)
    key_piece = lax.all_gather(prompt_key_value, "pool", axis=0, tiled=True)
    key_count = key_piece.shape[0]
    running_max = jnp.full((row_count, kv_heads, query_group_width), -1e30, jnp.float32)
    scores = (
        jnp.einsum(
            "thgd,shd->thgs",
            query_matrix,
            key_piece[..., :head_size],
            preferred_element_type=jnp.float32,
        )
        * score_scale
    )
    key_positions = jnp.arange(key_count, dtype=jnp.int32)
    allowed = (own_segments[:, None] == segment_ids[None, :]) & (
        key_positions[None, :] <= own_positions[:, None]
    )
    allowed = allowed[:, None, None, :]
    block_max = jnp.max(jnp.where(allowed, scores, -1e30), axis=-1)
    new_max = jnp.maximum(running_max, block_max)
    weights = jnp.where(allowed, jnp.exp(scores - new_max[..., None]), 0.0)
    new_sum = jnp.sum(weights, axis=-1)
    new_out = jnp.einsum(
        "thgs,shd->thgd",
        weights.astype(jnp.bfloat16),
        key_piece[..., head_size:],
        preferred_element_type=jnp.float32,
    )
    softmax_state = (new_max, new_sum, new_out)
    select_entries = (
        (destinations[:, None, :] == my_index) & (slot_ranks[:, None, :] == slot_ids[None, :, None])
    ).astype(jnp.bfloat16)
    arrived = jnp.einsum(
        "pcb,pbf->pcf",
        select_entries,
        key_piece.reshape(pool_size, block_count, flat_size),
        preferred_element_type=jnp.float32,
    ).astype(jnp.bfloat16)
    running_max, running_sum, running_out = softmax_state
    pre_att = (
        (running_out / running_sum[..., None])
        .reshape(row_count, query_heads * head_size)
        .astype(jnp.bfloat16)
    )
    arrived = arrived.reshape(1, pool_size, capacity, block_size, kv_heads, 2 * head_size)
    request_count = decode_query.shape[1]
    cache_length = dec_cache.shape[1]
    live_mask = (jnp.arange(cache_length, dtype=jnp.int32)[None, :] < ctx_len[:, None])[
        :, None, None, :
    ]
    old_keys = dec_cache[..., :head_size]
    old_values = dec_cache[..., head_size:]
    outputs = []
    for step_index in range(2):
        query_rows = decode_query[step_index].reshape(
            request_count, kv_heads, query_group_width, head_size
        )
        old_scores = (
            jnp.einsum("rhgd,rchd->rhgc", query_rows, old_keys, preferred_element_type=jnp.float32)
            * score_scale
        )
        new_scores = (
            jnp.einsum(
                "rhgd,nrhd->rhgn",
                query_rows,
                dec_kv[: step_index + 1, ..., :head_size],
                preferred_element_type=jnp.float32,
            )
            * score_scale
        )
        row_max = jnp.maximum(
            jnp.max(jnp.where(live_mask, old_scores, -1e30), axis=-1, keepdims=True),
            jnp.max(new_scores, axis=-1, keepdims=True),
        )
        old_weights = jnp.where(live_mask, jnp.exp(old_scores - row_max), 0.0)
        new_weights = jnp.exp(new_scores - row_max)
        weight_total = jnp.sum(old_weights, axis=-1) + jnp.sum(new_weights, axis=-1)
        combined = jnp.einsum(
            "rhgc,rchd->rhgd",
            old_weights.astype(jnp.bfloat16),
            old_values,
            preferred_element_type=jnp.float32,
        )
        combined = combined + jnp.einsum(
            "rhgn,nrhd->rhgd",
            new_weights.astype(jnp.bfloat16),
            dec_kv[: step_index + 1, ..., head_size:],
            preferred_element_type=jnp.float32,
        )
        outputs.append(
            (combined / weight_total[..., None]).reshape(request_count, query_heads * head_size)
        )
    dec_att = jnp.stack(outputs).astype(jnp.bfloat16)
    dec_count = 2 * request_count
    att = jnp.concatenate([dec_att.reshape(dec_count, -1), pre_att], axis=0)
    half = row_count // 2
    chunks = ((0, dec_count), (dec_count, half), (dec_count + half, half))
    projected = project_all(att, out_weight, chunks)
    slot_members, _, columns = projected.shape
    pre_sum = projected[:, dec_count:].reshape(slot_members * row_count, columns)
    dec_sum = (
        projected[:, :dec_count]
        .reshape(slot_members, 2, request_count, columns)
        .transpose(1, 0, 2, 3)
        .reshape(2, slot_members * request_count, columns)
    )
    return (pre_sum, dec_sum, arrived)


def solution(mesh):
    return jax.shard_map(
        body,
        mesh=mesh,
        in_specs=(
            P(("groups", "pool"), "tensor"),
            P(("groups", "pool"), "tensor", None),
            P("groups"),
            P("groups", None),
            P(None, ("groups", "pool"), "tensor"),
            P(None, ("groups", "pool"), "tensor", None),
            P(("groups", "pool"), None, "tensor", None),
            P(("groups", "pool")),
            P("tensor", "pool"),
        ),
        out_specs=(
            P(("groups", "tensor"), "pool"),
            P(None, ("groups", "tensor"), "pool"),
            P(("groups", "pool"), None, None, None, "tensor", None),
        ),
        check_vma=False,
    )
```

```python
import functools
import math

import jax
import jax.numpy as jnp
from jax import lax
from jax.experimental import pallas as pl
from jax.experimental.pallas import tpu as pltpu
from jax.sharding import PartitionSpec as P

BLOCK_TOKENS = 16
MESH = pl.DeviceIdType.MESH
COLUMN_TILE = 512


def inner(rows, keys):
    return lax.dot_general(
        rows, keys, (((1,), (1,)), ((), ())), preferred_element_type=jnp.float32
    )


def layer_kernel(
    chunks,
    slot_members,
    scale,
    query_ref,
    kv_ref,
    bias_ref,
    dec_query_ref,
    dec_new_ref,
    ctx_ref,
    pick_ref,
    cache_ref,
    weight_ref,
    pre_ref,
    dec_ref,
    arrived_ref,
    gathered,
    weight,
    outgoing,
    landed,
    total,
    cache,
    held,
    query,
    dec_rows,
    load_sem,
    cache_sem,
    kv_send,
    kv_recv,
    ring_send,
    ring_recv,
    part_send,
    part_recv,
):
    pool = lax.axis_size("pool")
    tensor = lax.axis_size("tensor")
    group = lax.axis_index("groups")
    me = lax.axis_index("pool")
    lane = lax.axis_index("tensor")
    columns = weight_ref.shape[1]
    tile = min(COLUMN_TILE, columns)
    has_left = me > 0
    has_right = me < pool - 1

    requests = cache_ref.shape[0]
    kv_heads = kv_ref.shape[0]
    head_size = kv_ref.shape[-1] // 2
    group_size = query_ref.shape[1] // (kv_heads * head_size)
    back = held.shape[0] - pool
    dec_count = chunks[0][1]

    load_kv = pltpu.make_async_copy(kv_ref, held.at[back + me], load_sem.at[0])
    load_kv.start()

    @pl.loop(0, requests)
    def _(request):
        pltpu.make_async_copy(
            cache_ref.at[request], cache.at[request], cache_sem.at[request]
        ).start()

    load_query = pltpu.make_async_copy(query_ref, query, load_sem.at[1])
    load_query.start()
    load_weight = pltpu.make_async_copy(weight_ref, weight, load_sem.at[2])
    load_weight.start()
    for place in range(back):
        held[place] = jnp.zeros(held.shape[1:], held.dtype)

    barrier = pltpu.get_barrier_semaphore()

    @pl.when(has_left)
    def _():
        pl.semaphore_signal(barrier, inc=1, device_id=(group, me - 1, lane), device_id_type=MESH)

    @pl.when(has_right)
    def _():
        pl.semaphore_signal(barrier, inc=1, device_id=(group, me + 1, lane), device_id_type=MESH)

    for step in range(1, tensor):
        peer = lax.rem(lane + step, tensor)
        pl.semaphore_signal(barrier, inc=1, device_id=(group, me, peer), device_id_type=MESH)

    pl.semaphore_wait(
        barrier, has_left.astype(jnp.int32) + has_right.astype(jnp.int32) + tensor - 1
    )

    def ring_copy(member, chunk, way):
        start, size = chunks[chunk]
        block = gathered.at[member, pl.ds(start, size)]
        return pltpu.make_async_remote_copy(
            src_ref=block,
            dst_ref=block,
            send_sem=ring_send.at[way, member, chunk],
            recv_sem=ring_recv.at[member, chunk],
            device_id=(group, me - 1 if way == 0 else me + 1, lane),
            device_id_type=MESH,
        )

    def part_copy(member, chunk):
        start, size = chunks[chunk]
        target = member // slot_members
        return pltpu.make_async_remote_copy(
            src_ref=outgoing.at[member, pl.ds(start, size)],
            dst_ref=landed.at[lane, member % slot_members, pl.ds(start, size)],
            send_sem=part_send.at[member, chunk],
            recv_sem=part_recv.at[lane, member % slot_members, chunk],
            device_id=(group, me, target),
            device_id_type=MESH,
        )

    def arrived_copy(source, place, chunk):
        start, size = chunks[chunk]
        return pltpu.make_async_remote_copy(
            src_ref=outgoing.at[0, pl.ds(start, size)],
            dst_ref=landed.at[source, place, pl.ds(start, size)],
            send_sem=part_send.at[0, chunk],
            recv_sem=part_recv.at[source, place, chunk],
            device_id=(group, me, source),
            device_id_type=MESH,
        )

    def project(member, chunk):
        start, size = chunks[chunk]
        mine = member // slot_members == lane

        @pl.loop(0, columns // tile)
        def _(index):
            place = pl.ds(pl.multiple_of(index * tile, tile), tile)
            part = jnp.dot(
                gathered[member, pl.ds(start, size), :],
                weight[:, place],
                preferred_element_type=jnp.float32,
            )

            @pl.when(mine)
            def _():
                total[member % slot_members, pl.ds(start, size), place] = part

            @pl.when(jnp.logical_not(mine))
            def _():
                outgoing[member, pl.ds(start, size), place] = part.astype(jnp.bfloat16)

        @pl.when(jnp.logical_not(mine))
        def _():
            part_copy(member, chunk).start()

    def kv_copy(member, way):
        block = held.at[back + member]
        return pltpu.make_async_remote_copy(
            src_ref=block,
            dst_ref=block,
            send_sem=kv_send.at[way, member],
            recv_sem=kv_recv.at[member],
            device_id=(group, me - 1 if way == 0 else me + 1, lane),
            device_id_type=MESH,
        )

    def pass_kv(distance):
        @pl.when(me - distance >= 0)
        def _():
            kv_copy(me - distance, 1).wait_recv()

            @pl.when(has_right)
            def _():
                kv_copy(me - distance, 1).start()

        @pl.when(me + distance < pool)
        def _():
            kv_copy(me + distance, 0).wait_recv()

            @pl.when(has_left)
            def _():
                kv_copy(me + distance, 0).start()

    def send_own(chunk):
        @pl.when(has_left)
        def _():
            ring_copy(me, chunk, 0).start()

        @pl.when(has_right)
        def _():
            ring_copy(me, chunk, 1).start()

    load_kv.wait()

    @pl.when(has_right)
    def _():
        kv_copy(me, 1).start()

    @pl.when(has_left)
    def _():
        kv_copy(me, 0).start()

    @pl.loop(0, requests)
    def _(request):
        for distance in range(1, back + 1):
            @pl.when(request == requests * distance // (back + 1))
            def _():
                pass_kv(distance)

        pltpu.make_async_copy(
            cache_ref.at[request], cache.at[request], cache_sem.at[request]
        ).wait()
        if len(cache.shape) == 4:
            slots = cache.shape[1] * cache.shape[2]
            keys = cache[request, :, :, 0:head_size].reshape(slots, head_size)
            values = cache[request, :, :, head_size:].reshape(slots, head_size)
        else:
            slots = cache.shape[1]
            keys = cache[request, :, 0:head_size]
            values = cache[request, :, head_size:]
        rows = dec_query_ref[request]
        new_keys = dec_new_ref[request, :, 0:head_size]
        new_values = dec_new_ref[request, :, head_size:]
        row = lax.broadcasted_iota(jnp.int32, (rows.shape[0], 1), 0)
        row_head = (row // group_size) % kv_heads
        row_step = row // (group_size * kv_heads)
        slot = lax.broadcasted_iota(jnp.int32, (1, slots), 1)
        new_slot = lax.broadcasted_iota(jnp.int32, (1, new_keys.shape[0]), 1)
        live = (slot % kv_heads == row_head) & (slot < ctx_ref[request] * kv_heads)
        new_live = (new_slot % kv_heads == row_head) & (new_slot // kv_heads <= row_step)
        scores = jnp.where(live, inner(rows, keys) * scale, -1e30)
        new_scores = jnp.where(new_live, inner(rows, new_keys) * scale, -1e30)
        most = jnp.maximum(
            jnp.max(scores, axis=-1, keepdims=True), jnp.max(new_scores, axis=-1, keepdims=True)
        )
        weights = jnp.exp(scores - most)
        new_weights = jnp.exp(new_scores - most)
        amount = jnp.sum(weights, axis=-1, keepdims=True) + jnp.sum(
            new_weights, axis=-1, keepdims=True
        )
        mixed = jnp.dot(
            weights.astype(jnp.bfloat16), values, preferred_element_type=jnp.float32
        ) + jnp.dot(
            new_weights.astype(jnp.bfloat16), new_values, preferred_element_type=jnp.float32
        )
        dec_rows[request] = mixed / amount

    heads = kv_heads * group_size
    for head in range(heads):
        both = jnp.concatenate([dec_rows[:, head, :], dec_rows[:, heads + head, :]], axis=0)
        gathered[me, 0:dec_count, head * head_size : (head + 1) * head_size] = both.astype(
            jnp.bfloat16
        )
    send_own(0)

    load_query.wait()
    for chunk in range(1, len(chunks)):
        start, size = chunks[chunk]
        first = start - dec_count
        for kv_head in range(kv_heads):
            @pl.loop(0, group_size // 2)
            def _(pair):
                column = pl.multiple_of(
                    (kv_head * group_size + 2 * pair) * head_size, 2 * head_size
                )
                wide = query[pl.ds(first, size), pl.ds(column, 2 * head_size)]
                rows = jnp.concatenate([wide[:, :head_size], wide[:, head_size:]], axis=0)
                bias = bias_ref[pl.ds(first, size), :]
                scores = jnp.concatenate(
                    [
                        inner(rows, held[me + place, kv_head, :, :, 0:head_size].reshape(-1, head_size))
                        for place in range(back + 1)
                    ],
                    axis=1,
                ) * scale + jnp.concatenate([bias, bias], axis=0)
                weights = jnp.exp(scores - jnp.max(scores, axis=-1, keepdims=True))
                amount = jnp.sum(weights, axis=-1, keepdims=True)
                weights = weights.astype(jnp.bfloat16)
                width = bias.shape[1] // (back + 1)
                mixed = jnp.zeros(rows.shape, jnp.float32)
                for place in range(back + 1):
                    mixed = mixed + jnp.dot(
                        weights[:, place * width : (place + 1) * width],
                        held[me + place, kv_head, :, :, head_size:].reshape(-1, head_size),
                        preferred_element_type=jnp.float32,
                    )
                mixed = (mixed / amount).astype(jnp.bfloat16)
                gathered[me, pl.ds(start, size), pl.ds(column, 2 * head_size)] = jnp.concatenate(
                    [mixed[:size], mixed[size:]], axis=1
                )
        send_own(chunk)

    load_weight.wait()

    @pl.loop(0, pool)
    def _(distance):
        left = me - distance
        right = me + distance
        use_left = left >= 0
        use_right = jnp.logical_and(right < pool, distance > 0)

        @pl.when(distance > back)
        def _():
            pass_kv(distance)

        for chunk in range(len(chunks)):
            @pl.when(jnp.logical_and(use_left, distance > 0))
            def _():
                ring_copy(left, chunk, 1).wait_recv()

                @pl.when(has_right)
                def _():
                    ring_copy(left, chunk, 1).start()

            @pl.when(use_right)
            def _():
                ring_copy(right, chunk, 0).wait_recv()

                @pl.when(has_left)
                def _():
                    ring_copy(right, chunk, 0).start()

            @pl.when(use_left)
            def _():
                project(left, chunk)

            @pl.when(use_right)
            def _():
                project(right, chunk)

    capacity = arrived_ref.shape[1]

    @pl.loop(0, pool)
    def _(source):
        for slot in range(capacity):
            choice = pick_ref[source * capacity + slot]
            for kv_head in range(kv_heads):
                block = held[back + source, kv_head, jnp.maximum(choice, 0)]
                arrived_ref[source, slot, kv_head] = jnp.where(
                    choice >= 0, block, jnp.zeros_like(block)
                )

    for place in range(slot_members):
        for chunk in range(len(chunks)):
            start, size = chunks[chunk]
            for step in range(1, tensor):
                arrived_copy(lax.rem(lane + step, tensor), place, chunk).wait_recv()

            @pl.loop(0, columns // tile)
            def _(index):
                span = pl.ds(pl.multiple_of(index * tile, tile), tile)
                value = total[place, pl.ds(start, size), span]
                for step in range(1, tensor):
                    source = lax.rem(lane + step, tensor)
                    value = value + landed[source, place, pl.ds(start, size), span].astype(
                        jnp.float32
                    )
                if chunk == 0:
                    dec_ref[place, :, span] = value.astype(jnp.bfloat16)
                else:
                    pre_ref[place, pl.ds(start - dec_count, size), span] = value.astype(
                        jnp.bfloat16
                    )

    @pl.loop(0, pool)
    def _(member):
        for chunk in range(len(chunks)):
            @pl.when(jnp.logical_and(has_left, member >= me))
            def _():
                if chunk == 0:
                    kv_copy(member, 0).wait_send()
                ring_copy(member, chunk, 0).wait_send()

            @pl.when(jnp.logical_and(has_right, member <= me))
            def _():
                if chunk == 0:
                    kv_copy(member, 1).wait_send()
                ring_copy(member, chunk, 1).wait_send()

            @pl.when(member // slot_members != lane)
            def _():
                part_copy(member, chunk).wait_send()


def attend_and_project(
    prompt_query, kv_blocks, bias, dec_query, dec_new, ctx_len, picks, dec_cache, out_weight,
    chunks, scale
):
    pool = lax.axis_size("pool")
    tensor = lax.axis_size("tensor")
    row_count, depth = prompt_query.shape
    rows = sum(size for _, size in chunks)
    columns = out_weight.shape[1]
    slot_members = pool // tensor
    count = len(chunks)
    back = bias.shape[1] // row_count - 1
    kv_heads, _, block_size, width = kv_blocks.shape
    requests = dec_cache.shape[0]
    capacity = picks.shape[0] // pool
    vmem = pl.BlockSpec(memory_space=pltpu.VMEM)
    smem = pl.BlockSpec(memory_space=pltpu.SMEM)
    hbm = pl.BlockSpec(memory_space=pl.ANY)
    return pl.pallas_call(
        functools.partial(layer_kernel, chunks, slot_members, scale),
        out_shape=(
            jax.ShapeDtypeStruct((slot_members, row_count, columns), jnp.bfloat16),
            jax.ShapeDtypeStruct((slot_members, chunks[0][1], columns), jnp.bfloat16),
            jax.ShapeDtypeStruct((pool, capacity, kv_heads, block_size, width), jnp.bfloat16),
        ),
        in_specs=[hbm, hbm, vmem, vmem, vmem, smem, smem, hbm, hbm],
        out_specs=(vmem, vmem, vmem),
        scratch_shapes=[
            pltpu.VMEM((pool, rows, depth), jnp.bfloat16),
            pltpu.VMEM((depth, columns), jnp.bfloat16),
            pltpu.VMEM((pool, rows, columns), jnp.bfloat16),
            pltpu.VMEM((tensor, slot_members, rows, columns), jnp.bfloat16),
            pltpu.VMEM((slot_members, rows, columns), jnp.float32),
            pltpu.VMEM(dec_cache.shape, jnp.bfloat16),
            pltpu.VMEM((back + pool,) + kv_blocks.shape, jnp.bfloat16),
            pltpu.VMEM(prompt_query.shape, jnp.bfloat16),
            pltpu.VMEM(dec_query.shape, jnp.float32),
            pltpu.SemaphoreType.DMA((3,)),
            pltpu.SemaphoreType.DMA((requests,)),
            pltpu.SemaphoreType.DMA((2, pool)),
            pltpu.SemaphoreType.DMA((pool,)),
            pltpu.SemaphoreType.DMA((2, pool, count)),
            pltpu.SemaphoreType.DMA((pool, count)),
            pltpu.SemaphoreType.DMA((pool, count)),
            pltpu.SemaphoreType.DMA((tensor, slot_members, count)),
        ],
        compiler_params=pltpu.CompilerParams(
            collective_id=0, has_side_effects=True, vmem_limit_bytes=58 * 1024 * 1024
        ),
    )(prompt_query, kv_blocks, bias, dec_query, dec_new, ctx_len, picks, dec_cache, out_weight)


def block_ranks(destinations):
    item_count = destinations.shape[-1]
    same_dest = destinations[..., :, None] == destinations[..., None, :]
    earlier = (
        jnp.arange(item_count, dtype=jnp.int32)[None, :]
        < jnp.arange(item_count, dtype=jnp.int32)[:, None]
    )
    return jnp.sum(jnp.where(same_dest & earlier, 1, 0), axis=-1).astype(jnp.int32)


def body(
    prompt_query,
    prompt_key_value,
    segment_ids,
    block_dest,
    decode_query,
    dec_kv,
    dec_cache,
    ctx_len,
    out_weight,
):
    row_count = prompt_query.shape[0]
    kv_heads = prompt_key_value.shape[1]
    head_size = prompt_key_value.shape[2] // 2
    query_heads = prompt_query.shape[1] // head_size
    group_size = query_heads // kv_heads
    scale = 1.0 / math.sqrt(head_size)
    pool_size = lax.axis_size("pool")
    my_index = lax.axis_index("pool")
    block_count = row_count // BLOCK_TOKENS
    capacity = max(2, 2 * block_count // pool_size)
    request_count = decode_query.shape[1]
    cache_length = dec_cache.shape[1]
    kv_blocks = prompt_key_value.transpose(1, 0, 2).reshape(
        kv_heads, block_count, BLOCK_TOKENS, 2 * head_size
    )

    most = pool_size * row_count // 2
    back = -(-(most - 1) // row_count)
    own_start = my_index * row_count
    own_positions = own_start + jnp.arange(row_count, dtype=jnp.int32)
    own_segments = lax.dynamic_slice_in_dim(segment_ids, own_start, row_count, 0)
    window = (back + 1) * row_count
    key_positions = own_start - back * row_count + jnp.arange(window, dtype=jnp.int32)
    padded = jnp.concatenate([jnp.full((back * row_count,), -1, jnp.int32), segment_ids])
    key_segments = lax.dynamic_slice_in_dim(padded, own_start, window, 0)
    allowed = (own_segments[:, None] == key_segments[None, :]) & (
        key_positions[None, :] <= own_positions[:, None]
    )
    bias = jnp.where(allowed, 0.0, -1e30).astype(jnp.float32)

    destinations = block_dest[:, 0].reshape(pool_size, block_count)
    slot_ranks = block_ranks(destinations)
    slot_ids = jnp.arange(capacity, dtype=jnp.int32)
    chosen = (destinations[:, None, :] == my_index) & (
        slot_ranks[:, None, :] == slot_ids[None, :, None]
    )
    picks = jnp.max(
        jnp.where(chosen, jnp.arange(block_count, dtype=jnp.int32)[None, None, :], -1), axis=-1
    ).reshape(-1)

    dec_query = (
        decode_query.reshape(2, request_count, query_heads, head_size)
        .transpose(1, 0, 2, 3)
        .reshape(request_count, 2 * query_heads, head_size)
    )
    dec_new = dec_kv.transpose(1, 0, 2, 3).reshape(request_count, 2 * kv_heads, 2 * head_size)
    dec_new = jnp.pad(dec_new, ((0, 0), (0, 16 - 2 * kv_heads), (0, 0)))
    if kv_heads == 1:
        dec_cache = dec_cache.reshape(request_count, cache_length, 2 * head_size)
    dec_count = 2 * request_count
    half = row_count // 2
    chunks = ((0, dec_count), (dec_count, half), (dec_count + half, half))
    pre, dec, arrived = attend_and_project(
        prompt_query, kv_blocks, bias, dec_query, dec_new, ctx_len, picks, dec_cache, out_weight,
        chunks, scale
    )
    slot_members, _, columns = pre.shape
    return (
        pre.reshape(slot_members * row_count, columns),
        dec.reshape(slot_members, 2, request_count, columns)
        .transpose(1, 0, 2, 3)
        .reshape(2, slot_members * request_count, columns),
        arrived.transpose(0, 1, 3, 2, 4)[None],
    )


def solution(mesh):
    return jax.shard_map(
        body,
        mesh=mesh,
        in_specs=(
            P(("groups", "pool"), "tensor"),
            P(("groups", "pool"), "tensor", None),
            P("groups"),
            P("groups", None),
            P(None, ("groups", "pool"), "tensor"),
            P(None, ("groups", "pool"), "tensor", None),
            P(("groups", "pool"), None, "tensor", None),
            P(("groups", "pool")),
            P("tensor", "pool"),
        ),
        out_specs=(
            P(("groups", "tensor"), "pool"),
            P(None, ("groups", "tensor"), "pool"),
            P(("groups", "pool"), None, None, None, "tensor", None),
        ),
        check_vma=False,
    )
```

```python
import functools
import math

import jax
import jax.numpy as jnp
from jax import lax
from jax.experimental import pallas as pl
from jax.experimental.pallas import tpu as pltpu
from jax.sharding import PartitionSpec as P

BLOCK_TOKENS = 16
MESH = pl.DeviceIdType.MESH
COLUMN_TILE = 512


def inner(rows, keys):
    return lax.dot_general(
        rows, keys, (((1,), (1,)), ((), ())), preferred_element_type=jnp.float32
    )


def layer_kernel(
    chunks,
    slot_members,
    scale,
    query_ref,
    kv_ref,
    bias_ref,
    dec_query_ref,
    dec_new_ref,
    ctx_ref,
    pick_ref,
    cache_ref,
    weight_ref,
    pre_ref,
    dec_ref,
    arrived_ref,
    gathered,
    weight,
    outgoing,
    landed,
    total,
    cache,
    held,
    query,
    dec_rows,
    load_sem,
    cache_sem,
    kv_send,
    kv_recv,
    ring_send,
    ring_recv,
    part_send,
    part_recv,
):
    pool = lax.axis_size("pool")
    tensor = lax.axis_size("tensor")
    group = lax.axis_index("groups")
    me = lax.axis_index("pool")
    lane = lax.axis_index("tensor")
    columns = weight_ref.shape[1]
    tile = min(COLUMN_TILE, columns)
    has_left = me > 0
    has_right = me < pool - 1

    requests = cache_ref.shape[0]
    kv_heads = kv_ref.shape[0]
    head_size = kv_ref.shape[-1] // 2
    group_size = query_ref.shape[1] // (kv_heads * head_size)
    back = held.shape[0] - pool
    dec_chunk = len(chunks) - 1
    dec_start, dec_count = chunks[dec_chunk]

    load_kv = pltpu.make_async_copy(kv_ref, held.at[back + me], load_sem.at[0])
    load_kv.start()

    @pl.loop(0, requests)
    def _(request):
        pltpu.make_async_copy(
            cache_ref.at[request], cache.at[request], cache_sem.at[request]
        ).start()

    load_query = pltpu.make_async_copy(query_ref, query, load_sem.at[1])
    load_query.start()
    load_weight = pltpu.make_async_copy(weight_ref, weight, load_sem.at[2])
    load_weight.start()
    for place in range(back):
        held[place] = jnp.zeros(held.shape[1:], held.dtype)

    barrier = pltpu.get_barrier_semaphore()

    @pl.when(has_left)
    def _():
        pl.semaphore_signal(barrier, inc=1, device_id=(group, me - 1, lane), device_id_type=MESH)

    @pl.when(has_right)
    def _():
        pl.semaphore_signal(barrier, inc=1, device_id=(group, me + 1, lane), device_id_type=MESH)

    for step in range(1, tensor):
        peer = lax.rem(lane + step, tensor)
        pl.semaphore_signal(barrier, inc=1, device_id=(group, me, peer), device_id_type=MESH)

    pl.semaphore_wait(
        barrier, has_left.astype(jnp.int32) + has_right.astype(jnp.int32) + tensor - 1
    )

    def ring_copy(member, chunk, way):
        start, size = chunks[chunk]
        block = gathered.at[member, pl.ds(start, size)]
        return pltpu.make_async_remote_copy(
            src_ref=block,
            dst_ref=block,
            send_sem=ring_send.at[way, member, chunk],
            recv_sem=ring_recv.at[member, chunk],
            device_id=(group, me - 1 if way == 0 else me + 1, lane),
            device_id_type=MESH,
        )

    def part_copy(member, chunk):
        start, size = chunks[chunk]
        target = member // slot_members
        return pltpu.make_async_remote_copy(
            src_ref=outgoing.at[member, pl.ds(start, size)],
            dst_ref=landed.at[lane, member % slot_members, pl.ds(start, size)],
            send_sem=part_send.at[member, chunk],
            recv_sem=part_recv.at[lane, member % slot_members, chunk],
            device_id=(group, me, target),
            device_id_type=MESH,
        )

    def arrived_copy(source, place, chunk):
        start, size = chunks[chunk]
        return pltpu.make_async_remote_copy(
            src_ref=outgoing.at[0, pl.ds(start, size)],
            dst_ref=landed.at[source, place, pl.ds(start, size)],
            send_sem=part_send.at[0, chunk],
            recv_sem=part_recv.at[source, place, chunk],
            device_id=(group, me, source),
            device_id_type=MESH,
        )

    def project(member, chunk):
        start, size = chunks[chunk]
        mine = member // slot_members == lane

        @pl.loop(0, columns // tile)
        def _(index):
            place = pl.ds(pl.multiple_of(index * tile, tile), tile)
            part = jnp.dot(
                gathered[member, pl.ds(start, size), :],
                weight[:, place],
                preferred_element_type=jnp.float32,
            )

            @pl.when(mine)
            def _():
                total[member % slot_members, pl.ds(start, size), place] = part

            @pl.when(jnp.logical_not(mine))
            def _():
                outgoing[member, pl.ds(start, size), place] = part.astype(jnp.bfloat16)

        @pl.when(jnp.logical_not(mine))
        def _():
            part_copy(member, chunk).start()

    def kv_copy(member, way):
        block = held.at[back + member]
        return pltpu.make_async_remote_copy(
            src_ref=block,
            dst_ref=block,
            send_sem=kv_send.at[way, member],
            recv_sem=kv_recv.at[member],
            device_id=(group, me - 1 if way == 0 else me + 1, lane),
            device_id_type=MESH,
        )

    def pass_kv(distance):
        @pl.when(me - distance >= 0)
        def _():
            kv_copy(me - distance, 1).wait_recv()

            @pl.when(has_right)
            def _():
                kv_copy(me - distance, 1).start()

        @pl.when(me + distance < pool)
        def _():
            kv_copy(me + distance, 0).wait_recv()

            @pl.when(has_left)
            def _():
                kv_copy(me + distance, 0).start()

    def send_own(chunk):
        @pl.when(has_left)
        def _():
            ring_copy(me, chunk, 0).start()

        @pl.when(has_right)
        def _():
            ring_copy(me, chunk, 1).start()

    load_kv.wait()

    @pl.when(has_right)
    def _():
        kv_copy(me, 1).start()

    @pl.when(has_left)
    def _():
        kv_copy(me, 0).start()

    def attend_request(request):
        pltpu.make_async_copy(
            cache_ref.at[request], cache.at[request], cache_sem.at[request]
        ).wait()
        if len(cache.shape) == 4:
            slots = cache.shape[1] * cache.shape[2]
            keys = cache[request, :, :, 0:head_size].reshape(slots, head_size)
            values = cache[request, :, :, head_size:].reshape(slots, head_size)
        else:
            slots = cache.shape[1]
            keys = cache[request, :, 0:head_size]
            values = cache[request, :, head_size:]
        rows = dec_query_ref[request]
        new_keys = dec_new_ref[request, :, 0:head_size]
        new_values = dec_new_ref[request, :, head_size:]
        row = lax.broadcasted_iota(jnp.int32, (rows.shape[0], 1), 0)
        row_head = (row // group_size) % kv_heads
        row_step = row // (group_size * kv_heads)
        slot = lax.broadcasted_iota(jnp.int32, (1, slots), 1)
        new_slot = lax.broadcasted_iota(jnp.int32, (1, new_keys.shape[0]), 1)
        live = (slot % kv_heads == row_head) & (slot < ctx_ref[request] * kv_heads)
        new_live = (new_slot % kv_heads == row_head) & (new_slot // kv_heads <= row_step)
        scores = jnp.where(live, inner(rows, keys) * scale, -1e30)
        new_scores = jnp.where(new_live, inner(rows, new_keys) * scale, -1e30)
        most = jnp.maximum(
            jnp.max(scores, axis=-1, keepdims=True), jnp.max(new_scores, axis=-1, keepdims=True)
        )
        weights = jnp.exp(scores - most)
        new_weights = jnp.exp(new_scores - most)
        amount = jnp.sum(weights, axis=-1, keepdims=True) + jnp.sum(
            new_weights, axis=-1, keepdims=True
        )
        mixed = jnp.dot(
            weights.astype(jnp.bfloat16), values, preferred_element_type=jnp.float32
        ) + jnp.dot(
            new_weights.astype(jnp.bfloat16), new_values, preferred_element_type=jnp.float32
        )
        dec_rows[request] = mixed / amount

    early = requests * 2 // 3

    @pl.loop(0, early)
    def _(request):
        for distance in range(1, back + 1):
            @pl.when(request == early * distance // back - 1)
            def _():
                pass_kv(distance)

        attend_request(request)

    load_query.wait()
    for chunk in range(dec_chunk):
        start, size = chunks[chunk]
        for kv_head in range(kv_heads):
            @pl.loop(0, group_size // 2)
            def _(pair):
                column = pl.multiple_of(
                    (kv_head * group_size + 2 * pair) * head_size, 2 * head_size
                )
                wide = query[pl.ds(start, size), pl.ds(column, 2 * head_size)]
                rows = jnp.concatenate([wide[:, :head_size], wide[:, head_size:]], axis=0)
                bias = bias_ref[pl.ds(start, size), :]
                scores = jnp.concatenate(
                    [
                        inner(rows, held[me + place, kv_head, :, :, 0:head_size].reshape(-1, head_size))
                        for place in range(back + 1)
                    ],
                    axis=1,
                ) * scale + jnp.concatenate([bias, bias], axis=0)
                weights = jnp.exp(scores - jnp.max(scores, axis=-1, keepdims=True))
                amount = jnp.sum(weights, axis=-1, keepdims=True)
                weights = weights.astype(jnp.bfloat16)
                width = bias.shape[1] // (back + 1)
                mixed = jnp.zeros(rows.shape, jnp.float32)
                for place in range(back + 1):
                    mixed = mixed + jnp.dot(
                        weights[:, place * width : (place + 1) * width],
                        held[me + place, kv_head, :, :, head_size:].reshape(-1, head_size),
                        preferred_element_type=jnp.float32,
                    )
                mixed = (mixed / amount).astype(jnp.bfloat16)
                gathered[me, pl.ds(start, size), pl.ds(column, 2 * head_size)] = jnp.concatenate(
                    [mixed[:size], mixed[size:]], axis=1
                )
        send_own(chunk)

    @pl.loop(early, requests)
    def _(request):
        attend_request(request)

    heads = kv_heads * group_size
    for head in range(heads):
        both = jnp.concatenate([dec_rows[:, head, :], dec_rows[:, heads + head, :]], axis=0)
        gathered[me, dec_start : dec_start + dec_count, head * head_size : (head + 1) * head_size] = both.astype(
            jnp.bfloat16
        )
    send_own(dec_chunk)

    load_weight.wait()

    @pl.loop(0, pool)
    def _(distance):
        left = me - distance
        right = me + distance
        use_left = left >= 0
        use_right = jnp.logical_and(right < pool, distance > 0)

        @pl.when(distance > back)
        def _():
            pass_kv(distance)

        for chunk in range(len(chunks)):
            @pl.when(jnp.logical_and(use_left, distance > 0))
            def _():
                ring_copy(left, chunk, 1).wait_recv()

                @pl.when(has_right)
                def _():
                    ring_copy(left, chunk, 1).start()

            @pl.when(use_right)
            def _():
                ring_copy(right, chunk, 0).wait_recv()

                @pl.when(has_left)
                def _():
                    ring_copy(right, chunk, 0).start()

            @pl.when(use_left)
            def _():
                project(left, chunk)

            @pl.when(use_right)
            def _():
                project(right, chunk)

    capacity = arrived_ref.shape[1]

    @pl.loop(0, pool)
    def _(source):
        for slot in range(capacity):
            choice = pick_ref[source * capacity + slot]
            for kv_head in range(kv_heads):
                block = held[back + source, kv_head, jnp.maximum(choice, 0)]
                arrived_ref[source, slot, kv_head] = jnp.where(
                    choice >= 0, block, jnp.zeros_like(block)
                )

    for place in range(slot_members):
        for chunk in range(len(chunks)):
            start, size = chunks[chunk]
            for step in range(1, tensor):
                arrived_copy(lax.rem(lane + step, tensor), place, chunk).wait_recv()

            @pl.loop(0, columns // tile)
            def _(index):
                span = pl.ds(pl.multiple_of(index * tile, tile), tile)
                value = total[place, pl.ds(start, size), span]
                for step in range(1, tensor):
                    source = lax.rem(lane + step, tensor)
                    value = value + landed[source, place, pl.ds(start, size), span].astype(
                        jnp.float32
                    )
                if chunk == dec_chunk:
                    dec_ref[place, :, span] = value.astype(jnp.bfloat16)
                else:
                    pre_ref[place, pl.ds(start, size), span] = value.astype(
                        jnp.bfloat16
                    )

    @pl.loop(0, pool)
    def _(member):
        for chunk in range(len(chunks)):
            @pl.when(jnp.logical_and(has_left, member >= me))
            def _():
                if chunk == 0:
                    kv_copy(member, 0).wait_send()
                ring_copy(member, chunk, 0).wait_send()

            @pl.when(jnp.logical_and(has_right, member <= me))
            def _():
                if chunk == 0:
                    kv_copy(member, 1).wait_send()
                ring_copy(member, chunk, 1).wait_send()

            @pl.when(member // slot_members != lane)
            def _():
                part_copy(member, chunk).wait_send()


def attend_and_project(
    prompt_query, kv_blocks, bias, dec_query, dec_new, ctx_len, picks, dec_cache, out_weight,
    chunks, scale
):
    pool = lax.axis_size("pool")
    tensor = lax.axis_size("tensor")
    row_count, depth = prompt_query.shape
    rows = sum(size for _, size in chunks)
    columns = out_weight.shape[1]
    slot_members = pool // tensor
    count = len(chunks)
    back = bias.shape[1] // row_count - 1
    kv_heads, _, block_size, width = kv_blocks.shape
    requests = dec_cache.shape[0]
    capacity = picks.shape[0] // pool
    vmem = pl.BlockSpec(memory_space=pltpu.VMEM)
    smem = pl.BlockSpec(memory_space=pltpu.SMEM)
    hbm = pl.BlockSpec(memory_space=pl.ANY)
    return pl.pallas_call(
        functools.partial(layer_kernel, chunks, slot_members, scale),
        out_shape=(
            jax.ShapeDtypeStruct((slot_members, row_count, columns), jnp.bfloat16),
            jax.ShapeDtypeStruct((slot_members, chunks[-1][1], columns), jnp.bfloat16),
            jax.ShapeDtypeStruct((pool, capacity, kv_heads, block_size, width), jnp.bfloat16),
        ),
        in_specs=[hbm, hbm, vmem, vmem, vmem, smem, smem, hbm, hbm],
        out_specs=(vmem, vmem, vmem),
        scratch_shapes=[
            pltpu.VMEM((pool, rows, depth), jnp.bfloat16),
            pltpu.VMEM((depth, columns), jnp.bfloat16),
            pltpu.VMEM((pool, rows, columns), jnp.bfloat16),
            pltpu.VMEM((tensor, slot_members, rows, columns), jnp.bfloat16),
            pltpu.VMEM((slot_members, rows, columns), jnp.float32),
            pltpu.VMEM(dec_cache.shape, jnp.bfloat16),
            pltpu.VMEM((back + pool,) + kv_blocks.shape, jnp.bfloat16),
            pltpu.VMEM(prompt_query.shape, jnp.bfloat16),
            pltpu.VMEM(dec_query.shape, jnp.float32),
            pltpu.SemaphoreType.DMA((3,)),
            pltpu.SemaphoreType.DMA((requests,)),
            pltpu.SemaphoreType.DMA((2, pool)),
            pltpu.SemaphoreType.DMA((pool,)),
            pltpu.SemaphoreType.DMA((2, pool, count)),
            pltpu.SemaphoreType.DMA((pool, count)),
            pltpu.SemaphoreType.DMA((pool, count)),
            pltpu.SemaphoreType.DMA((tensor, slot_members, count)),
        ],
        compiler_params=pltpu.CompilerParams(
            collective_id=0, has_side_effects=True, vmem_limit_bytes=58 * 1024 * 1024
        ),
    )(prompt_query, kv_blocks, bias, dec_query, dec_new, ctx_len, picks, dec_cache, out_weight)


def block_ranks(destinations):
    item_count = destinations.shape[-1]
    same_dest = destinations[..., :, None] == destinations[..., None, :]
    earlier = (
        jnp.arange(item_count, dtype=jnp.int32)[None, :]
        < jnp.arange(item_count, dtype=jnp.int32)[:, None]
    )
    return jnp.sum(jnp.where(same_dest & earlier, 1, 0), axis=-1).astype(jnp.int32)


def body(
    prompt_query,
    prompt_key_value,
    segment_ids,
    block_dest,
    decode_query,
    dec_kv,
    dec_cache,
    ctx_len,
    out_weight,
):
    row_count = prompt_query.shape[0]
    kv_heads = prompt_key_value.shape[1]
    head_size = prompt_key_value.shape[2] // 2
    query_heads = prompt_query.shape[1] // head_size
    group_size = query_heads // kv_heads
    scale = 1.0 / math.sqrt(head_size)
    pool_size = lax.axis_size("pool")
    my_index = lax.axis_index("pool")
    block_count = row_count // BLOCK_TOKENS
    capacity = max(2, 2 * block_count // pool_size)
    request_count = decode_query.shape[1]
    cache_length = dec_cache.shape[1]
    kv_blocks = prompt_key_value.transpose(1, 0, 2).reshape(
        kv_heads, block_count, BLOCK_TOKENS, 2 * head_size
    )

    most = pool_size * row_count // 2
    back = -(-(most - 1) // row_count)
    own_start = my_index * row_count
    own_positions = own_start + jnp.arange(row_count, dtype=jnp.int32)
    own_segments = lax.dynamic_slice_in_dim(segment_ids, own_start, row_count, 0)
    window = (back + 1) * row_count
    key_positions = own_start - back * row_count + jnp.arange(window, dtype=jnp.int32)
    padded = jnp.concatenate([jnp.full((back * row_count,), -1, jnp.int32), segment_ids])
    key_segments = lax.dynamic_slice_in_dim(padded, own_start, window, 0)
    allowed = (own_segments[:, None] == key_segments[None, :]) & (
        key_positions[None, :] <= own_positions[:, None]
    )
    bias = jnp.where(allowed, 0.0, -1e30).astype(jnp.float32)

    destinations = block_dest[:, 0].reshape(pool_size, block_count)
    slot_ranks = block_ranks(destinations)
    slot_ids = jnp.arange(capacity, dtype=jnp.int32)
    chosen = (destinations[:, None, :] == my_index) & (
        slot_ranks[:, None, :] == slot_ids[None, :, None]
    )
    picks = jnp.max(
        jnp.where(chosen, jnp.arange(block_count, dtype=jnp.int32)[None, None, :], -1), axis=-1
    ).reshape(-1)

    dec_query = (
        decode_query.reshape(2, request_count, query_heads, head_size)
        .transpose(1, 0, 2, 3)
        .reshape(request_count, 2 * query_heads, head_size)
    )
    dec_new = dec_kv.transpose(1, 0, 2, 3).reshape(request_count, 2 * kv_heads, 2 * head_size)
    dec_new = jnp.pad(dec_new, ((0, 0), (0, 16 - 2 * kv_heads), (0, 0)))
    if kv_heads == 1:
        dec_cache = dec_cache.reshape(request_count, cache_length, 2 * head_size)
    dec_count = 2 * request_count
    half = row_count // 2
    chunks = ((0, half), (half, half), (row_count, dec_count))
    pre, dec, arrived = attend_and_project(
        prompt_query, kv_blocks, bias, dec_query, dec_new, ctx_len, picks, dec_cache, out_weight,
        chunks, scale
    )
    slot_members, _, columns = pre.shape
    return (
        pre.reshape(slot_members * row_count, columns),
        dec.reshape(slot_members, 2, request_count, columns)
        .transpose(1, 0, 2, 3)
        .reshape(2, slot_members * request_count, columns),
        arrived.transpose(0, 1, 3, 2, 4)[None],
    )


def solution(mesh):
    return jax.shard_map(
        body,
        mesh=mesh,
        in_specs=(
            P(("groups", "pool"), "tensor"),
            P(("groups", "pool"), "tensor", None),
            P("groups"),
            P("groups", None),
            P(None, ("groups", "pool"), "tensor"),
            P(None, ("groups", "pool"), "tensor", None),
            P(("groups", "pool"), None, "tensor", None),
            P(("groups", "pool")),
            P("tensor", "pool"),
        ),
        out_specs=(
            P(("groups", "tensor"), "pool"),
            P(None, ("groups", "tensor"), "pool"),
            P(("groups", "pool"), None, None, None, "tensor", None),
        ),
        check_vma=False,
    )
```

```python
import functools
import math

import jax
import jax.numpy as jnp
from jax import lax
from jax.experimental import pallas as pl
from jax.experimental.pallas import tpu as pltpu
from jax.sharding import PartitionSpec as P

BLOCK_TOKENS = 16
MESH = pl.DeviceIdType.MESH
COLUMN_TILE = 512


def inner(rows, keys):
    return lax.dot_general(
        rows, keys, (((1,), (1,)), ((), ())), preferred_element_type=jnp.float32
    )


def layer_kernel(
    chunks,
    slot_members,
    scale,
    query_ref,
    kv_ref,
    bias_ref,
    dec_query_ref,
    dec_new_ref,
    ctx_ref,
    pick_ref,
    cache_ref,
    weight_ref,
    pre_ref,
    dec_ref,
    arrived_ref,
    gathered,
    weight,
    outgoing,
    landed,
    paired,
    total,
    cache,
    held,
    query,
    dec_rows,
    load_sem,
    cache_sem,
    kv_send,
    kv_recv,
    ring_send,
    ring_recv,
    pair_send,
    pair_recv,
    part_send,
    part_recv,
):
    pool = lax.axis_size("pool")
    tensor = lax.axis_size("tensor")
    group = lax.axis_index("groups")
    me = lax.axis_index("pool")
    lane = lax.axis_index("tensor")
    columns = weight_ref.shape[1]
    half = columns // 2
    tile = min(COLUMN_TILE, half)
    core = lane % 2
    partner = lane - core + (1 - core)
    has_left = me > 0
    has_right = me < pool - 1

    requests = cache_ref.shape[0]
    kv_heads = kv_ref.shape[0]
    head_size = kv_ref.shape[-1] // 2
    group_size = query_ref.shape[1] // (kv_heads * head_size)
    back = held.shape[0] - pool
    dec_chunk = len(chunks) - 1
    dec_start, dec_count = chunks[dec_chunk]

    load_kv = pltpu.make_async_copy(kv_ref, held.at[back + me], load_sem.at[0])
    load_kv.start()

    @pl.loop(0, requests)
    def _(request):
        pltpu.make_async_copy(
            cache_ref.at[request], cache.at[request], cache_sem.at[request]
        ).start()

    load_query = pltpu.make_async_copy(query_ref, query, load_sem.at[1])
    load_query.start()
    load_weight = pltpu.make_async_copy(weight_ref, weight, load_sem.at[2])
    load_weight.start()
    for place in range(back):
        held[place] = jnp.zeros(held.shape[1:], held.dtype)

    barrier = pltpu.get_barrier_semaphore()

    @pl.when(has_left)
    def _():
        pl.semaphore_signal(barrier, inc=1, device_id=(group, me - 1, lane), device_id_type=MESH)

    @pl.when(has_right)
    def _():
        pl.semaphore_signal(barrier, inc=1, device_id=(group, me + 1, lane), device_id_type=MESH)

    for step in range(1, tensor):
        peer = lax.rem(lane + step, tensor)
        pl.semaphore_signal(barrier, inc=1, device_id=(group, me, peer), device_id_type=MESH)

    pl.semaphore_wait(
        barrier, has_left.astype(jnp.int32) + has_right.astype(jnp.int32) + tensor - 1
    )

    def ring_copy(member, chunk, way):
        start, size = chunks[chunk]
        block = gathered.at[member, pl.ds(start, size)]
        return pltpu.make_async_remote_copy(
            src_ref=block,
            dst_ref=block,
            send_sem=ring_send.at[way, member, chunk],
            recv_sem=ring_recv.at[member, chunk],
            device_id=(group, me - 1 if way == 0 else me + 1, lane),
            device_id_type=MESH,
        )

    def pair_copy(member, chunk):
        start, size = chunks[chunk]
        return pltpu.make_async_remote_copy(
            src_ref=outgoing.at[1 - core, member, pl.ds(start, size)],
            dst_ref=paired.at[member, pl.ds(start, size)],
            send_sem=pair_send.at[member, chunk],
            recv_sem=pair_recv.at[member, chunk],
            device_id=(group, me, partner),
            device_id_type=MESH,
        )

    def part_copy(side, member, chunk):
        start, size = chunks[chunk]
        place = member % slot_members
        return pltpu.make_async_remote_copy(
            src_ref=outgoing.at[side, member, pl.ds(start, size)],
            dst_ref=landed.at[lane, side, place, pl.ds(start, size)],
            send_sem=part_send.at[side, member, chunk],
            recv_sem=part_recv.at[lane, side, place, chunk],
            device_id=(group, me, member // slot_members),
            device_id_type=MESH,
        )

    def arrived_copy(source, side, place, chunk):
        start, size = chunks[chunk]
        return pltpu.make_async_remote_copy(
            src_ref=outgoing.at[side, 0, pl.ds(start, size)],
            dst_ref=landed.at[source, side, place, pl.ds(start, size)],
            send_sem=part_send.at[side, 0, chunk],
            recv_sem=part_recv.at[source, side, place, chunk],
            device_id=(group, me, source),
            device_id_type=MESH,
        )

    def project(member, chunk):
        start, size = chunks[chunk]
        mine = member // slot_members == lane

        @pl.loop(0, columns // tile)
        def _(index):
            place = pl.ds(pl.multiple_of(index * tile, tile), tile)
            part = jnp.dot(
                gathered[member, pl.ds(start, size), :],
                weight[:, place],
                preferred_element_type=jnp.float32,
            )

            @pl.when(mine)
            def _():
                total[member % slot_members, pl.ds(start, size), place] = part

            @pl.when(jnp.logical_not(mine))
            def _():
                outgoing[
                    index * tile // half,
                    member,
                    pl.ds(start, size),
                    pl.ds(pl.multiple_of(index * tile % half, tile), tile),
                ] = part.astype(jnp.bfloat16)

        @pl.when(member // slot_members == partner)
        def _():
            part_copy(0, member, chunk).start()
            part_copy(1, member, chunk).start()

        @pl.when(member // slot_members // 2 != lane // 2)
        def _():
            pair_copy(member, chunk).start()
            pair_copy(member, chunk).wait_recv()
            outgoing[core, member, pl.ds(start, size), :] = (
                outgoing[core, member, pl.ds(start, size), :].astype(jnp.float32)
                + paired[member, pl.ds(start, size), :].astype(jnp.float32)
            ).astype(jnp.bfloat16)
            part_copy(core, member, chunk).start()

    def kv_copy(member, way):
        block = held.at[back + member]
        return pltpu.make_async_remote_copy(
            src_ref=block,
            dst_ref=block,
            send_sem=kv_send.at[way, member],
            recv_sem=kv_recv.at[member],
            device_id=(group, me - 1 if way == 0 else me + 1, lane),
            device_id_type=MESH,
        )

    def pass_kv(distance):
        @pl.when(me - distance >= 0)
        def _():
            kv_copy(me - distance, 1).wait_recv()

            @pl.when(has_right)
            def _():
                kv_copy(me - distance, 1).start()

        @pl.when(me + distance < pool)
        def _():
            kv_copy(me + distance, 0).wait_recv()

            @pl.when(has_left)
            def _():
                kv_copy(me + distance, 0).start()

    def send_own(chunk):
        @pl.when(has_left)
        def _():
            ring_copy(me, chunk, 0).start()

        @pl.when(has_right)
        def _():
            ring_copy(me, chunk, 1).start()

    load_kv.wait()

    @pl.when(has_right)
    def _():
        kv_copy(me, 1).start()

    @pl.when(has_left)
    def _():
        kv_copy(me, 0).start()

    def attend_request(request):
        pltpu.make_async_copy(
            cache_ref.at[request], cache.at[request], cache_sem.at[request]
        ).wait()
        if len(cache.shape) == 4:
            slots = cache.shape[1] * cache.shape[2]
            keys = cache[request, :, :, 0:head_size].reshape(slots, head_size)
            values = cache[request, :, :, head_size:].reshape(slots, head_size)
        else:
            slots = cache.shape[1]
            keys = cache[request, :, 0:head_size]
            values = cache[request, :, head_size:]
        rows = dec_query_ref[request]
        new_keys = dec_new_ref[request, :, 0:head_size]
        new_values = dec_new_ref[request, :, head_size:]
        row = lax.broadcasted_iota(jnp.int32, (rows.shape[0], 1), 0)
        row_head = (row // group_size) % kv_heads
        row_step = row // (group_size * kv_heads)
        slot = lax.broadcasted_iota(jnp.int32, (1, slots), 1)
        new_slot = lax.broadcasted_iota(jnp.int32, (1, new_keys.shape[0]), 1)
        live = (slot % kv_heads == row_head) & (slot < ctx_ref[request] * kv_heads)
        new_live = (new_slot % kv_heads == row_head) & (new_slot // kv_heads <= row_step)
        scores = jnp.where(live, inner(rows, keys) * scale, -1e30)
        new_scores = jnp.where(new_live, inner(rows, new_keys) * scale, -1e30)
        most = jnp.maximum(
            jnp.max(scores, axis=-1, keepdims=True), jnp.max(new_scores, axis=-1, keepdims=True)
        )
        weights = jnp.exp(scores - most)
        new_weights = jnp.exp(new_scores - most)
        amount = jnp.sum(weights, axis=-1, keepdims=True) + jnp.sum(
            new_weights, axis=-1, keepdims=True
        )
        mixed = jnp.dot(
            weights.astype(jnp.bfloat16), values, preferred_element_type=jnp.float32
        ) + jnp.dot(
            new_weights.astype(jnp.bfloat16), new_values, preferred_element_type=jnp.float32
        )
        dec_rows[request] = mixed / amount

    early = requests * 2 // 3

    @pl.loop(0, early)
    def _(request):
        for distance in range(1, back + 1):
            @pl.when(request == early * distance // back - 1)
            def _():
                pass_kv(distance)

        attend_request(request)

    load_query.wait()
    for chunk in range(dec_chunk):
        start, size = chunks[chunk]
        for kv_head in range(kv_heads):
            @pl.loop(0, group_size // 2)
            def _(pair):
                column = pl.multiple_of(
                    (kv_head * group_size + 2 * pair) * head_size, 2 * head_size
                )
                wide = query[pl.ds(start, size), pl.ds(column, 2 * head_size)]
                rows = jnp.concatenate([wide[:, :head_size], wide[:, head_size:]], axis=0)
                bias = bias_ref[pl.ds(start, size), :]
                scores = jnp.concatenate(
                    [
                        inner(rows, held[me + place, kv_head, :, :, 0:head_size].reshape(-1, head_size))
                        for place in range(back + 1)
                    ],
                    axis=1,
                ) * scale + jnp.concatenate([bias, bias], axis=0)
                weights = jnp.exp(scores - jnp.max(scores, axis=-1, keepdims=True))
                amount = jnp.sum(weights, axis=-1, keepdims=True)
                weights = weights.astype(jnp.bfloat16)
                width = bias.shape[1] // (back + 1)
                mixed = jnp.zeros(rows.shape, jnp.float32)
                for place in range(back + 1):
                    mixed = mixed + jnp.dot(
                        weights[:, place * width : (place + 1) * width],
                        held[me + place, kv_head, :, :, head_size:].reshape(-1, head_size),
                        preferred_element_type=jnp.float32,
                    )
                mixed = (mixed / amount).astype(jnp.bfloat16)
                gathered[me, pl.ds(start, size), pl.ds(column, 2 * head_size)] = jnp.concatenate(
                    [mixed[:size], mixed[size:]], axis=1
                )
        send_own(chunk)

    @pl.loop(early, requests)
    def _(request):
        attend_request(request)

    heads = kv_heads * group_size
    for head in range(heads):
        both = jnp.concatenate([dec_rows[:, head, :], dec_rows[:, heads + head, :]], axis=0)
        gathered[me, dec_start : dec_start + dec_count, head * head_size : (head + 1) * head_size] = both.astype(
            jnp.bfloat16
        )
    send_own(dec_chunk)

    load_weight.wait()

    @pl.loop(0, pool)
    def _(distance):
        left = me - distance
        right = me + distance
        use_left = left >= 0
        use_right = jnp.logical_and(right < pool, distance > 0)

        @pl.when(distance > back)
        def _():
            pass_kv(distance)

        for chunk in range(len(chunks)):
            @pl.when(jnp.logical_and(use_left, distance > 0))
            def _():
                ring_copy(left, chunk, 1).wait_recv()

                @pl.when(has_right)
                def _():
                    ring_copy(left, chunk, 1).start()

            @pl.when(use_right)
            def _():
                ring_copy(right, chunk, 0).wait_recv()

                @pl.when(has_left)
                def _():
                    ring_copy(right, chunk, 0).start()

            @pl.when(use_left)
            def _():
                project(left, chunk)

            @pl.when(use_right)
            def _():
                project(right, chunk)

    capacity = arrived_ref.shape[1]

    @pl.loop(0, pool)
    def _(source):
        for slot in range(capacity):
            choice = pick_ref[source * capacity + slot]
            for kv_head in range(kv_heads):
                block = held[back + source, kv_head, jnp.maximum(choice, 0)]
                arrived_ref[source, slot, kv_head] = jnp.where(
                    choice >= 0, block, jnp.zeros_like(block)
                )

    for place in range(slot_members):
        for chunk in range(len(chunks)):
            start, size = chunks[chunk]
            for side in range(2):
                arrived_copy(partner, side, place, chunk).wait_recv()
                for step in range(1, tensor // 2):
                    chip = lax.rem(lane // 2 + step, tensor // 2)
                    arrived_copy(2 * chip + side, side, place, chunk).wait_recv()

            @pl.loop(0, columns // tile)
            def _(index):
                span = pl.ds(pl.multiple_of(index * tile, tile), tile)
                value = total[place, pl.ds(start, size), span]
                side = index * tile // half
                inside = pl.ds(pl.multiple_of(index * tile % half, tile), tile)
                value = value + landed[partner, side, place, pl.ds(start, size), inside].astype(
                    jnp.float32
                )
                for step in range(1, tensor // 2):
                    chip = lax.rem(lane // 2 + step, tensor // 2)
                    value = value + landed[
                        2 * chip + side, side, place, pl.ds(start, size), inside
                    ].astype(jnp.float32)
                if chunk == dec_chunk:
                    dec_ref[place, :, span] = value.astype(jnp.bfloat16)
                else:
                    pre_ref[place, pl.ds(start, size), span] = value.astype(
                        jnp.bfloat16
                    )

    @pl.loop(0, pool)
    def _(member):
        for chunk in range(len(chunks)):
            @pl.when(jnp.logical_and(has_left, member >= me))
            def _():
                if chunk == 0:
                    kv_copy(member, 0).wait_send()
                ring_copy(member, chunk, 0).wait_send()

            @pl.when(jnp.logical_and(has_right, member <= me))
            def _():
                if chunk == 0:
                    kv_copy(member, 1).wait_send()
                ring_copy(member, chunk, 1).wait_send()

            @pl.when(member // slot_members == partner)
            def _():
                part_copy(0, member, chunk).wait_send()
                part_copy(1, member, chunk).wait_send()

            @pl.when(member // slot_members // 2 != lane // 2)
            def _():
                pair_copy(member, chunk).wait_send()
                part_copy(core, member, chunk).wait_send()


def attend_and_project(
    prompt_query, kv_blocks, bias, dec_query, dec_new, ctx_len, picks, dec_cache, out_weight,
    chunks, scale
):
    pool = lax.axis_size("pool")
    tensor = lax.axis_size("tensor")
    row_count, depth = prompt_query.shape
    rows = sum(size for _, size in chunks)
    columns = out_weight.shape[1]
    slot_members = pool // tensor
    count = len(chunks)
    back = bias.shape[1] // row_count - 1
    kv_heads, _, block_size, width = kv_blocks.shape
    requests = dec_cache.shape[0]
    capacity = picks.shape[0] // pool
    vmem = pl.BlockSpec(memory_space=pltpu.VMEM)
    smem = pl.BlockSpec(memory_space=pltpu.SMEM)
    hbm = pl.BlockSpec(memory_space=pl.ANY)
    return pl.pallas_call(
        functools.partial(layer_kernel, chunks, slot_members, scale),
        out_shape=(
            jax.ShapeDtypeStruct((slot_members, row_count, columns), jnp.bfloat16),
            jax.ShapeDtypeStruct((slot_members, chunks[-1][1], columns), jnp.bfloat16),
            jax.ShapeDtypeStruct((pool, capacity, kv_heads, block_size, width), jnp.bfloat16),
        ),
        in_specs=[hbm, hbm, vmem, vmem, vmem, smem, smem, hbm, hbm],
        out_specs=(vmem, vmem, vmem),
        scratch_shapes=[
            pltpu.VMEM((pool, rows, depth), jnp.bfloat16),
            pltpu.VMEM((depth, columns), jnp.bfloat16),
            pltpu.VMEM((2, pool, rows, columns // 2), jnp.bfloat16),
            pltpu.VMEM((tensor, 2, slot_members, rows, columns // 2), jnp.bfloat16),
            pltpu.VMEM((pool, rows, columns // 2), jnp.bfloat16),
            pltpu.VMEM((slot_members, rows, columns), jnp.float32),
            pltpu.VMEM(dec_cache.shape, jnp.bfloat16),
            pltpu.VMEM((back + pool,) + kv_blocks.shape, jnp.bfloat16),
            pltpu.VMEM(prompt_query.shape, jnp.bfloat16),
            pltpu.VMEM(dec_query.shape, jnp.float32),
            pltpu.SemaphoreType.DMA((3,)),
            pltpu.SemaphoreType.DMA((requests,)),
            pltpu.SemaphoreType.DMA((2, pool)),
            pltpu.SemaphoreType.DMA((pool,)),
            pltpu.SemaphoreType.DMA((2, pool, count)),
            pltpu.SemaphoreType.DMA((pool, count)),
            pltpu.SemaphoreType.DMA((pool, count)),
            pltpu.SemaphoreType.DMA((pool, count)),
            pltpu.SemaphoreType.DMA((2, pool, count)),
            pltpu.SemaphoreType.DMA((tensor, 2, slot_members, count)),
        ],
        compiler_params=pltpu.CompilerParams(
            collective_id=0, has_side_effects=True, vmem_limit_bytes=58 * 1024 * 1024
        ),
    )(prompt_query, kv_blocks, bias, dec_query, dec_new, ctx_len, picks, dec_cache, out_weight)


def block_ranks(destinations):
    item_count = destinations.shape[-1]
    same_dest = destinations[..., :, None] == destinations[..., None, :]
    earlier = (
        jnp.arange(item_count, dtype=jnp.int32)[None, :]
        < jnp.arange(item_count, dtype=jnp.int32)[:, None]
    )
    return jnp.sum(jnp.where(same_dest & earlier, 1, 0), axis=-1).astype(jnp.int32)


def body(
    prompt_query,
    prompt_key_value,
    segment_ids,
    block_dest,
    decode_query,
    dec_kv,
    dec_cache,
    ctx_len,
    out_weight,
):
    row_count = prompt_query.shape[0]
    kv_heads = prompt_key_value.shape[1]
    head_size = prompt_key_value.shape[2] // 2
    query_heads = prompt_query.shape[1] // head_size
    group_size = query_heads // kv_heads
    scale = 1.0 / math.sqrt(head_size)
    pool_size = lax.axis_size("pool")
    my_index = lax.axis_index("pool")
    block_count = row_count // BLOCK_TOKENS
    capacity = max(2, 2 * block_count // pool_size)
    request_count = decode_query.shape[1]
    cache_length = dec_cache.shape[1]
    kv_blocks = prompt_key_value.transpose(1, 0, 2).reshape(
        kv_heads, block_count, BLOCK_TOKENS, 2 * head_size
    )

    most = pool_size * row_count // 2
    back = -(-(most - 1) // row_count)
    own_start = my_index * row_count
    own_positions = own_start + jnp.arange(row_count, dtype=jnp.int32)
    own_segments = lax.dynamic_slice_in_dim(segment_ids, own_start, row_count, 0)
    window = (back + 1) * row_count
    key_positions = own_start - back * row_count + jnp.arange(window, dtype=jnp.int32)
    padded = jnp.concatenate([jnp.full((back * row_count,), -1, jnp.int32), segment_ids])
    key_segments = lax.dynamic_slice_in_dim(padded, own_start, window, 0)
    allowed = (own_segments[:, None] == key_segments[None, :]) & (
        key_positions[None, :] <= own_positions[:, None]
    )
    bias = jnp.where(allowed, 0.0, -1e30).astype(jnp.float32)

    destinations = block_dest[:, 0].reshape(pool_size, block_count)
    slot_ranks = block_ranks(destinations)
    slot_ids = jnp.arange(capacity, dtype=jnp.int32)
    chosen = (destinations[:, None, :] == my_index) & (
        slot_ranks[:, None, :] == slot_ids[None, :, None]
    )
    picks = jnp.max(
        jnp.where(chosen, jnp.arange(block_count, dtype=jnp.int32)[None, None, :], -1), axis=-1
    ).reshape(-1)

    dec_query = (
        decode_query.reshape(2, request_count, query_heads, head_size)
        .transpose(1, 0, 2, 3)
        .reshape(request_count, 2 * query_heads, head_size)
    )
    dec_new = dec_kv.transpose(1, 0, 2, 3).reshape(request_count, 2 * kv_heads, 2 * head_size)
    dec_new = jnp.pad(dec_new, ((0, 0), (0, 16 - 2 * kv_heads), (0, 0)))
    if kv_heads == 1:
        dec_cache = dec_cache.reshape(request_count, cache_length, 2 * head_size)
    dec_count = 2 * request_count
    half = row_count // 2
    chunks = ((0, half), (half, half), (row_count, dec_count))
    pre, dec, arrived = attend_and_project(
        prompt_query, kv_blocks, bias, dec_query, dec_new, ctx_len, picks, dec_cache, out_weight,
        chunks, scale
    )
    slot_members, _, columns = pre.shape
    return (
        pre.reshape(slot_members * row_count, columns),
        dec.reshape(slot_members, 2, request_count, columns)
        .transpose(1, 0, 2, 3)
        .reshape(2, slot_members * request_count, columns),
        arrived.transpose(0, 1, 3, 2, 4)[None],
    )


def solution(mesh):
    return jax.shard_map(
        body,
        mesh=mesh,
        in_specs=(
            P(("groups", "pool"), "tensor"),
            P(("groups", "pool"), "tensor", None),
            P("groups"),
            P("groups", None),
            P(None, ("groups", "pool"), "tensor"),
            P(None, ("groups", "pool"), "tensor", None),
            P(("groups", "pool"), None, "tensor", None),
            P(("groups", "pool")),
            P("tensor", "pool"),
        ),
        out_specs=(
            P(("groups", "tensor"), "pool"),
            P(None, ("groups", "tensor"), "pool"),
            P(("groups", "pool"), None, None, None, "tensor", None),
        ),
        check_vma=False,
    )
```
